32 devices in a mesh: row: 2 (over x), col: 2 (over y), dp: 8 (over z, core).
Axes of the slice: x: 2, y: 2, z: 4, core: 2. Of those that a mesh axis runs over, the one named last changes fastest.
Arguments:
- features: bfloat16 [8, 48, 48, 1024], P('dp', 'row', 'col'), may hold values from -6 to 6
- cotangent: bfloat16 [8, 48, 48, 256], P('dp', 'row', 'col'), may hold values from -0.09375 to 0.09375
- w_point: bfloat16 [1024, 256], replicated, may hold values from -0.1875 to 0.1875
- w_rate_a: bfloat16 [3, 3, 1024, 256], replicated, may hold values from -0.0625 to 0.0625
- w_rate_b: bfloat16 [3, 3, 1024, 256], replicated, may hold values from -0.0625 to 0.0625
- w_rate_c: bfloat16 [3, 3, 1024, 256], replicated, may hold values from -0.0625 to 0.0625
- w_proj: bfloat16 [1024, 256], replicated, may hold values from -0.1875 to 0.1875
- bucket_slot: int32 [176], replicated, may hold values from 0 to 183, as said below
Outputs:
- owned_grads: float32 [184, 16384], P('dp', ('row', 'col'))
The draws below stay inside these ranges and needn't reach their ends.
Inputs may be any that keep to these rules, and one draw needn't show every extreme that they name: Distinct slot numbers, one for each of the 176 slices; slice s belongs to data replica bucket_slot[s] // 23. In every draw all 23 slots of some replica are taken. Rows of owned_grads that no slice names are zero.
All inputs are finite; a program needn't handle non-finite values.
Results may differ from the reference program's by a relative error of at most 0.0043.
Values may be sent and summed in bfloat16 or wider, within the bound.
A program may use at most 192 MiB of HBM per device.

```python
import jax
import jax.numpy as jnp
from jax import lax

CIN = 1024
CO = 256
CAT = 1024
RATE_A = 6
RATE_B = 12
RATE_C = 18
H = 48
W = 48
SROWS = 64
NSLICE = 176
CAP = 23
SLOTS = 184
N_DP = 8


def draw_bucket_slot(key, part):
    key_owner = jax.random.fold_in(key, 11)
    key_score = jax.random.fold_in(key, 12)
    key_order = jax.random.fold_in(key, 13)
    full_owner = jax.random.randint(key_owner, (), 0, SLOTS // CAP)
    slot_ids = jnp.arange(SLOTS, dtype=jnp.int32)
    owners = slot_ids // CAP
    score = jax.random.randint(key_score, (SLOTS,), 0, 1 << 20)
    score = jnp.where(owners == full_owner, 1 << 21, score) * SLOTS + slot_ids
    unused, chosen = lax.top_k(score, NSLICE)
    order = jax.random.permutation(key_order, NSLICE)
    return chosen[order].astype(jnp.int32)


def block_scale(key, dims, cuts, least, top_value):
    factor_of = 1.0
    for axis_at, shards_of in cuts:
        heights = jax.random.uniform(jax.random.fold_in(jax.random.fold_in(key, 6), axis_at), (shards_of,), jnp.float32, least / len(cuts), top_value / len(cuts))
        factor_of = factor_of * jnp.repeat(jnp.exp(heights), dims[axis_at] // shards_of).reshape((-1,) + (1,) * (len(dims) - 1 - axis_at))
    return factor_of


def bell_draw(rng, extent, spread, reach, cuts=(), held_as=jnp.bfloat16):
    array = jax.random.normal(rng, extent, jnp.float32) * spread
    if len(cuts) > 0:
        array = block_scale(rng, extent, cuts, -0.22, 0.18) * array
    return jnp.clip(array, min=-reach, max=reach).astype(held_as)


def setup_inputs(seed: int = 0) -> dict:
    key_list = jax.random.split(jax.random.key(seed), 9)
    features = bell_draw(key_list[0], (N_DP, H, W, CIN), 1.0, 6.0, ((0, 8), (1, 2), (2, 2)))
    cotangent = bell_draw(key_list[1], (N_DP, H, W, CO), 0.006, 0.09375, ((0, 8), (1, 2), (2, 2)))
    w_point = bell_draw(key_list[2], (CIN, CO), CIN ** -0.5, 0.1875)
    w_rate_a = bell_draw(key_list[3], (3, 3, CIN, CO), (9 * CIN) ** -0.5, 0.0625)
    w_rate_b = bell_draw(key_list[4], (3, 3, CIN, CO), (9 * CIN) ** -0.5, 0.0625)
    w_rate_c = bell_draw(key_list[5], (3, 3, CIN, CO), (9 * CIN) ** -0.5, 0.0625)
    w_proj = bell_draw(key_list[6], (CAT, CO), CAT ** -0.5, 0.1875)
    bucket_slot = draw_bucket_slot(jax.random.fold_in(key_list[8], 71), 0)
    return dict(features=features, cotangent=cotangent, w_point=w_point, w_rate_a=w_rate_a, w_rate_b=w_rate_b, w_rate_c=w_rate_c, w_proj=w_proj, bucket_slot=bucket_slot)


def silu_slope(value):
    sig = jax.nn.sigmoid(value)
    return sig * (1.0 + value * (1.0 - sig))


def contract_pixels(left, right):
    return lax.dot_general(left, right, (((0,), (0,)), ((), ())), preferred_element_type=jnp.float32)


def image_grads(image, upstream, w_point, kernels, w_proj):
    rows_img, cols_img, chans = image.shape
    pixels = rows_img * cols_img
    width = RATE_C
    padded = jnp.pad(image, ((width, width), (width, width), (0, 0)))

    def window(rate, above, across):
        top = width + above * rate
        left = width + across * rate
        return padded[top:top + rows_img, left:left + cols_img].reshape(pixels, chans)

    rates = (RATE_A, RATE_B, RATE_C)
    centre = window(0, 0, 0)
    pre_list = [jnp.dot(centre, w_point, preferred_element_type=jnp.float32)]
    for rate, kernel in zip(rates, kernels):
        total = jnp.zeros((pixels, CO), jnp.float32)
        for above in range(3):
            for across in range(3):
                total = total + jnp.dot(window(rate, above - 1, across - 1), kernel[above, across], preferred_element_type=jnp.float32)
        pre_list.append(total)
    joined = jnp.concatenate([jax.nn.silu(pre) for pre in pre_list], 1).astype(jnp.bfloat16)
    proj_pre = jnp.dot(joined, w_proj, preferred_element_type=jnp.float32)
    g_proj = (upstream.reshape(pixels, CO).astype(jnp.float32) * silu_slope(proj_pre)).astype(jnp.bfloat16)
    pieces = [contract_pixels(joined, g_proj)]
    d_joined = lax.dot_general(g_proj, w_proj, (((1,), (1,)), ((), ())), preferred_element_type=jnp.float32)
    for index in (0, 3):
        pre = pre_list[index]
        d_pre = (d_joined[:, index * CO:(index + 1) * CO] * silu_slope(pre)).astype(jnp.bfloat16)
        if index == 0:
            pieces.append(contract_pixels(centre, d_pre))
        else:
            for above in range(3):
                for across in range(3):
                    pieces.append(contract_pixels(window(RATE_C, above - 1, across - 1), d_pre))
    return jnp.concatenate(pieces, 0)


def reference(features, cotangent, w_point, w_rate_a, w_rate_b, w_rate_c, w_proj, bucket_slot):
    kernels = (w_rate_a, w_rate_b, w_rate_c)

    def add_image(total, pair):
        return total + image_grads(pair[0], pair[1], w_point, kernels, w_proj), None

    start = jnp.zeros((CAT + 10 * CIN, CO), jnp.float32)
    total, unused = lax.scan(add_image, start, (features, cotangent))
    slices = total.reshape(NSLICE, SROWS * CO)
    return jnp.zeros((SLOTS, SROWS * CO), jnp.float32).at[bucket_slot].set(slices)
```

```python
import functools

import jax
import jax.numpy as jnp
from jax import lax
from jax.experimental import pallas as pl
from jax.experimental.pallas import tpu as pltpu
from jax.sharding import PartitionSpec as P

RATES = (18, 12, 6)
SPAN = {18: 0, 12: 18, 6: 30}
DIAG = {18: (0, 0), 12: (18, 0), 6: (0, 18)}
REACH = 18
SROWS = 64
MESH = pl.DeviceIdType.MESH
VMEM = pltpu.VMEM
BF16 = jnp.bfloat16
F32 = jnp.float32
LIMIT = 56 * 1024 * 1024


def silu_slope(value):
    sig = jax.nn.sigmoid(value)
    return sig * (1.0 + value * (1.0 - sig))


def forward_kernel(n, f_ref, wc_ref, wb_ref, wa_ref, wp_ref, own_ref, v_ref, h_ref, d_ref,
                   s_ref, t_ref, hs_ref, ds_ref):
    step = pl.program_id(0)
    row, col = lax.axis_index("row"), lax.axis_index("col")
    width = f_ref.shape[1]
    outs = wp_ref.shape[1]

    @pl.when(step == 0)
    def _():
        hs_ref[...] = jnp.zeros_like(hs_ref)
        ds_ref[...] = jnp.zeros_like(ds_ref)

    for index, (rate, w_ref) in enumerate(zip(RATES, (wc_ref, wb_ref, wa_ref))):
        tall = n + 2 * rate

        for tap in range(3):
            @pl.when(step == 3 * index + tap)
            def _(rate=rate, w_ref=w_ref, tap=tap, tall=tall):
                top = (2 - tap) * rate * n
                if tap == 0:
                    s_ref[:, : tall * n, :] = jnp.zeros((3, tall * n, outs), F32)
                for across in range(3):
                    s_ref[across, top : top + n * n, :] += jnp.dot(
                        f_ref[...], w_ref[0, across], preferred_element_type=F32
                    )

        @pl.when(step == 3 * index + 2)
        def _(rate=rate, tall=tall, index=index):
            t_ref[...] = jnp.zeros_like(t_ref)
            t_ref[:tall, n : 2 * n, :] = s_ref[1, : tall * n, :].reshape(tall, n, outs)
            t_ref[:tall, n + rate : 2 * n + rate, :] += s_ref[0, : tall * n, :].reshape(tall, n, outs)
            t_ref[:tall, n - rate : 2 * n - rate, :] += s_ref[2, : tall * n, :].reshape(tall, n, outs)
            own_ref[3 - index] = t_ref[rate : rate + n, n : 2 * n, :].reshape(n * n, outs)
            vtop = (1 - row) * (n + rate)
            at = SPAN[rate]
            drow, dcol = DIAG[rate]
            v_ref[at : at + rate] = t_ref[pl.ds(vtop, rate), n : 2 * n, :].astype(BF16)
            for side, left in ((0, 2 * n), (1, n - rate)):
                @pl.when(col == side)
                def _(left=left):
                    hs_ref[:, at : at + rate, :] = t_ref[rate : rate + n, left : left + rate, :]
                    ds_ref[drow : drow + rate, dcol : dcol + rate, :] = t_ref[
                        pl.ds(vtop, rate), left : left + rate, :
                    ]

    @pl.when(step == 9)
    def _():
        own_ref[0] = jnp.dot(f_ref[...], wp_ref[...], preferred_element_type=F32)
        h_ref[...] = hs_ref[...].astype(BF16)
        d_ref[...] = ds_ref[...].astype(BF16)


def forward(n, f, wc, wb, wa, wp):
    pix, chans = f.shape
    outs = wp.shape[1]
    whole = lambda shape: pl.BlockSpec(shape, lambda t: (0,) * len(shape))
    taps = lambda first: pl.BlockSpec(
        (1, 3, chans, outs), lambda t: (jnp.clip(t - first, 0, 2), 0, 0, 0)
    )
    shapes = [((4, pix, outs), F32), ((36, n, outs), BF16), ((n, 40, outs), BF16), ((30, n, outs), BF16)]
    return pl.pallas_call(
        functools.partial(forward_kernel, n),
        grid=(10,),
        out_shape=[jax.ShapeDtypeStruct(s, d) for s, d in shapes],
        in_specs=[whole((pix, chans)), taps(0), taps(3), taps(6), whole((chans, outs))],
        out_specs=[whole(s) for s, _ in shapes],
        scratch_shapes=[
            VMEM((3, (n + 36) * n, outs), F32),
            VMEM((n + 36, 3 * n, outs), F32),
            VMEM((n, 40, outs), F32),
            VMEM((30, n, outs), F32),
        ],
        compiler_params=pltpu.CompilerParams(vmem_limit_bytes=LIMIT),
        cost_estimate=pl.CostEstimate(flops=28 * 2 * pix * chans * outs, bytes_accessed=17_000_000, transcendentals=0),
    )(f, wc, wb, wa, wp)


def middle_kernel(n, own_ref, v_ref, h_ref, d_ref, cot_ref, wp_ref, joined_ref, g_ref, d0_ref, d3_ref, v3_ref,
                  acc_ref, hs_ref, ds_ref):
    row, col = lax.axis_index("row"), lax.axis_index("col")
    outs = cot_ref.shape[1]
    pix = n * n
    hs_ref[...] = h_ref[...].astype(F32)
    ds_ref[...] = d_ref[...].astype(F32)
    for index, rate in enumerate(RATES):
        k = 3 - index
        at = SPAN[rate]
        drow, dcol = DIAG[rate]
        vtop = (1 - row) * (n - rate)
        acc_ref[k] = own_ref[k].reshape(n, n, outs)
        acc_ref[k, pl.ds(vtop, rate)] += v_ref[at : at + rate].astype(F32)
        for side, left in ((0, n - rate), (1, 0)):
            @pl.when(col == side)
            def _(left=left):
                acc_ref[k, :, left : left + rate, :] += hs_ref[:, at : at + rate, :]
                acc_ref[k, pl.ds(vtop, rate), left : left + rate, :] += ds_ref[
                    drow : drow + rate, dcol : dcol + rate, :
                ]
    acc_ref[0] = own_ref[0].reshape(n, n, outs)
    for k in range(4):
        pre = acc_ref[k].reshape(pix, outs)
        joined_ref[:, k * outs : (k + 1) * outs] = (pre * jax.nn.sigmoid(pre)).astype(BF16)
    proj_pre = jnp.dot(joined_ref[...], wp_ref[...], preferred_element_type=F32)
    g_ref[...] = (cot_ref[...].astype(F32) * silu_slope(proj_pre)).astype(BF16)
    for k, out_ref in ((0, d0_ref), (3, d3_ref)):
        d_joined = lax.dot_general(
            g_ref[...], wp_ref[k * outs : (k + 1) * outs, :], (((1,), (1,)), ((), ())),
            preferred_element_type=F32,
        )
        out_ref[...] = (d_joined * silu_slope(acc_ref[k].reshape(pix, outs))).astype(BF16)
    v3_ref[...] = d3_ref[pl.ds(pl.multiple_of((1 - row) * ((n - REACH) * n), 16), REACH * n), :]


def middle(n, own, v, h, d, cot, wp):
    pix, outs = cot.shape
    chans = wp.shape[0]
    shapes = [(pix, chans), (pix, outs), (pix, outs), (pix, outs), (REACH * n, outs)]
    return pl.pallas_call(
        functools.partial(middle_kernel, n),
        out_shape=[jax.ShapeDtypeStruct(s, BF16) for s in shapes],
        in_specs=[pl.BlockSpec(memory_space=VMEM)] * 6,
        out_specs=[pl.BlockSpec(memory_space=VMEM)] * 5,
        scratch_shapes=[VMEM((4, n, n, outs), F32), VMEM(h.shape, F32), VMEM(d.shape, F32)],
        compiler_params=pltpu.CompilerParams(vmem_limit_bytes=LIMIT),
    )(own, v, h, d, cot, wp)


def grads_kernel(n, cap, bs_ref, f_ref, joined_ref, g_ref, d0_ref, d3_ref, v3_ref, h3_ref, c3_ref, keep_ref,
                 give_ref, p_ref, pb_ref, ft_ref):
    row, col = lax.axis_index("row"), lax.axis_index("col")
    core = lax.rem(lax.axis_index("dp"), 2)
    pix, outs = g_ref.shape
    chans = f_ref.shape[1]
    per = chans // SROWS
    part = SROWS // 4
    keep_ref[...] = jnp.zeros_like(keep_ref)
    give_ref[...] = jnp.zeros_like(give_ref)

    def place(piece, value):
        for s in range(per):
            slot = bs_ref[piece * per + s]
            owner = slot // cap
            for out_ref, side in ((keep_ref, core), (give_ref, 1 - core)):
                @pl.when(lax.rem(owner, 2) == side)
                def _(out_ref=out_ref):
                    for q in range(4):
                        at = s * SROWS + q * part
                        out_ref[owner // 2, q, slot % cap] = value[at : at + part, :].astype(out_ref.dtype)

    ft_ref[...] = joined_ref[...].T
    place(0, jnp.dot(ft_ref[...], g_ref[...], preferred_element_type=F32))
    ft_ref[...] = f_ref[...].T
    place(1, jnp.dot(ft_ref[...], d0_ref[...], preferred_element_type=F32))

    p_ref[...] = jnp.zeros_like(p_ref)
    p_ref[REACH : REACH + n, n : 2 * n, :] = d3_ref[...].astype(F32).reshape(n, n, outs)
    rtop = (1 - row) * (REACH + n)
    cleft = pl.multiple_of((1 - col) * 2 * n, 8)
    p_ref[pl.ds(rtop, REACH), n : 2 * n, :] = v3_ref[...].astype(F32).reshape(REACH, n, outs)
    p_ref[REACH : REACH + n, pl.ds(cleft, n), :] = h3_ref[...].astype(F32).reshape(n, n, outs)
    p_ref[pl.ds(rtop, REACH), pl.ds(cleft, n), :] = c3_ref[...].astype(F32).reshape(REACH, n, outs)
    tall = n + 2 * REACH
    for across in range(3):
        left = n - (across - 1) * REACH
        pb_ref[across] = p_ref[:, left : left + n, :].reshape(tall * n, outs).astype(BF16)

    def tap(t, carry):
        above, across = t // 3, t % 3
        start = pl.multiple_of((2 - above) * (REACH * n), 16)
        place(2 + t, jnp.dot(ft_ref[...], pb_ref[across, pl.ds(start, pix), :], preferred_element_type=F32))
        return carry

    lax.fori_loop(0, 9, tap, 0)


def grads(n, cap, pairs, bs, f, joined, g, d0, d3, v3, h3, c3):
    pix, chans = f.shape
    outs = g.shape[1]
    return pl.pallas_call(
        functools.partial(grads_kernel, n, cap),
        out_shape=[jax.ShapeDtypeStruct((pairs, 4, cap, SROWS // 4, outs), d) for d in (F32, BF16)],
        in_specs=[pl.BlockSpec(memory_space=pltpu.SMEM)] + [pl.BlockSpec(memory_space=VMEM)] * 8,
        out_specs=[pl.BlockSpec(memory_space=VMEM)] * 2,
        scratch_shapes=[
            VMEM((n + 2 * REACH, 3 * n, outs), F32),
            VMEM((3, (n + 2 * REACH) * n, outs), BF16),
            VMEM((chans, pix), BF16),
        ],
        compiler_params=pltpu.CompilerParams(vmem_limit_bytes=LIMIT),
    )(bs, f, joined, g, d0, d3, v3, h3, c3)


def reduce_kernel(pairs, half, keep_ref, give_ref, out_ref, r_ref, ax_ref, ay_ref, x1_ref, y1_ref, my_ref, mx_ref,
                  y2_ref, x2_ref, fin_ref, z_ref, send, recv):
    row, col, dp = lax.axis_index("row"), lax.axis_index("col"), lax.axis_index("dp")
    core, mine = lax.rem(dp, 2), dp // 2
    depth = keep_ref.shape[2]
    other = {"dp": mine * 2 + 1 - core}
    beside_x = {"row": 1 - row}
    beside_y = {"col": 1 - col}
    zs = [lax.rem(mine + j, pairs) for j in range(pairs)]
    along = [{"dp": zs[j] * 2 + core} for j in range(pairs)]

    barrier = pltpu.get_barrier_semaphore()
    partners = [other, beside_x, beside_y] + along[1:]
    for partner in partners:
        pl.semaphore_signal(barrier, inc=1, device_id=partner, device_id_type=MESH)
    pl.semaphore_wait(barrier, len(partners))

    def copy(kind, j, src, dst, where):
        return pltpu.make_async_remote_copy(
            src_ref=src, dst_ref=dst, send_sem=send.at[kind, j], recv_sem=recv.at[kind, j],
            device_id=where, device_id_type=MESH,
        )

    order = list(range(1, pairs)) + [0]
    low, high = pl.ds(0, half), pl.ds(half, depth - half)
    cores = {j: copy(0, j, give_ref.at[zs[j]], r_ref.at[j], other) for j in order}
    for j in order:
        cores[j].start()
    x1, y1, x2, y2, along_z = {}, {}, {}, {}, {}

    def pair(j, r, c, rows):
        return keep_ref[zs[j], r * 2 + c, rows, :] + r_ref[j, r * 2 + c, rows, :].astype(F32)

    def first(j):
        cores[j].wait_recv()
        for k in range(2):
            ax_ref[j, k] = pair(j, 1 - row, k, low).astype(BF16)
            ay_ref[j, k] = pair(j, k, 1 - col, high).astype(BF16)
        x1[j] = copy(1, j, ax_ref.at[j], x1_ref.at[j], beside_x)
        y1[j] = copy(2, j, ay_ref.at[j], y1_ref.at[j], beside_y)
        x1[j].start()
        y1[j].start()

    def second(j):
        x1[j].wait_recv()
        my_ref[j] = (pair(j, row, 1 - col, low) + x1_ref[j, 1 - col].astype(F32)).astype(BF16)
        y2[j] = copy(3, j, my_ref.at[j], y2_ref.at[j], beside_y)
        y2[j].start()
        y1[j].wait_recv()
        mx_ref[j] = (pair(j, 1 - row, col, high) + y1_ref[j, 1 - row].astype(F32)).astype(BF16)
        x2[j] = copy(4, j, mx_ref.at[j], x2_ref.at[j], beside_x)
        x2[j].start()

    def third(j):
        y2[j].wait_recv()
        x2[j].wait_recv()
        lower = pair(j, row, col, low) + x1_ref[j, col].astype(F32) + y2_ref[j].astype(F32)
        upper = pair(j, row, col, high) + y1_ref[j, row].astype(F32) + x2_ref[j].astype(F32)
        if j == 0:
            out_ref[low, :] = lower
            out_ref[high, :] = upper
        else:
            fin_ref[j, low, :] = lower.astype(BF16)
            fin_ref[j, high, :] = upper.astype(BF16)
            along_z[j] = copy(5, j, fin_ref.at[j], z_ref.at[j], along[j])
            along_z[j].start()

    for at in range(pairs + 2):
        if at < pairs:
            first(order[at])
        if 1 <= at <= pairs:
            second(order[at - 1])
        if at >= 2:
            third(order[at - 2])
    for j in order[:-1]:
        along_z[j].wait_recv()
        out_ref[...] += z_ref[j].astype(F32)
    for j in order:
        for group in (cores, x1, y1, x2, y2):
            group[j].wait_send()
        if j:
            along_z[j].wait_send()


def reduce_scatter(keep, give):
    pairs, quarters, depth, outs = keep.shape
    half = (depth // 16 + 1) // 2 * 16
    rest = depth - half
    buf = lambda *shape: VMEM(shape + (outs,), BF16)
    return pl.pallas_call(
        functools.partial(reduce_kernel, pairs, half),
        out_shape=jax.ShapeDtypeStruct((depth, outs), F32),
        in_specs=[pl.BlockSpec(memory_space=VMEM)] * 2,
        out_specs=pl.BlockSpec(memory_space=VMEM),
        scratch_shapes=[
            buf(pairs, quarters, depth),
            buf(pairs, 2, half),
            buf(pairs, 2, rest),
            buf(pairs, 2, half),
            buf(pairs, 2, rest),
            buf(pairs, half),
            buf(pairs, rest),
            buf(pairs, half),
            buf(pairs, rest),
            buf(pairs, depth),
            buf(pairs, depth),
            pltpu.SemaphoreType.DMA((6, pairs)),
            pltpu.SemaphoreType.DMA((6, pairs)),
        ],
        compiler_params=pltpu.CompilerParams(
            collective_id=0, has_side_effects=True, vmem_limit_bytes=LIMIT
        ),
    )(keep, give)


def shards(features, cotangent, w_point, w_rate_a, w_rate_b, w_rate_c, w_proj, bucket_slot):
    n = features.shape[1]
    chans = features.shape[3]
    outs = w_point.shape[1]
    pix = n * n
    f = features.reshape(pix, chans)
    cot = cotangent.reshape(pix, outs)
    swap = [(0, 1), (1, 0)]
    cross = [(i, 3 - i) for i in range(4)]
    replicas = lax.axis_size("dp")
    nslice = bucket_slot.shape[0]
    cap = nslice // replicas + 1
    own, v, h, d = forward(n, f, w_rate_c, w_rate_b, w_rate_a, w_point)
    d = lax.ppermute(d, ("row", "col"), cross)
    v = lax.ppermute(v, "row", swap)
    h = lax.ppermute(h, "col", swap)
    joined, g, d0, d3, v3 = middle(n, own, v, h, d, cot, w_proj)
    c3 = lax.ppermute(v3, ("row", "col"), cross)
    v3 = lax.ppermute(v3, "row", swap)
    h3 = lax.ppermute(d3, "col", swap)
    keep, give = grads(n, cap, replicas // 2, bucket_slot, f, joined, g, d0, d3, v3, h3, c3)
    shape = (replicas // 2, 4, cap * (SROWS // 4), outs)
    total = reduce_scatter(keep.reshape(shape), give.reshape(shape))
    return total.reshape(cap, SROWS // 4 * outs)


def solution(mesh):
    placed = (
        P("dp", "row", "col", None),
        P("dp", "row", "col", None),
        P(),
        P(),
        P(),
        P(),
        P(),
        P(),
    )
    return jax.shard_map(
        shards, mesh=mesh, in_specs=placed, out_specs=P("dp", ("row", "col")), check_vma=False
    )
```

```python
import functools

import jax
import jax.numpy as jnp
from jax import lax
from jax.experimental import pallas as pl
from jax.experimental.pallas import tpu as pltpu
from jax.sharding import PartitionSpec as P

RATES = (18, 12, 6)
REACH = 18
SROWS = 64
MESH = pl.DeviceIdType.MESH
VMEM = pltpu.VMEM
BF16 = jnp.bfloat16
F32 = jnp.float32
LIMIT = 56 * 1024 * 1024


def silu_slope(value):
    sig = jax.nn.sigmoid(value)
    return sig * (1.0 + value * (1.0 - sig))


def padded_rows(count):
    return -(-count // 16) * 16


def edge_sizes(n):
    v, h, d = {}, {}, {}
    tops = [0, 0, 0]
    for rate in RATES:
        for k, (table, size) in enumerate(((v, rate * n), (h, n * rate), (d, rate * rate))):
            table[rate] = pl.ds(tops[k], padded_rows(size))
            tops[k] += padded_rows(size)
    return (v, h, d), tops


def forward_kernel(n, f_ref, wc_ref, wb_ref, wa_ref, wp_ref, cot_ref, wq_ref, g01_ref, ft_ref, pb_ref,
                   s_ref, t_ref, acc_ref, strip, vs_ref, hs_ref, ds_ref, vr_ref, hr_ref, dr_ref,
                   joined_ref, jt_ref, g_ref, d0_ref, d3_ref, v3_ref, h3_ref, c3_ref, h3s_ref, c3s_ref,
                   send, recv):
    step = pl.program_id(0)
    row, col = lax.axis_index("row"), lax.axis_index("col")
    outs = wp_ref.shape[1]
    pix = n * n
    spans, unused = edge_sizes(n)

    def cut(src, top, rows, rate, lefts):
        for side, left in enumerate(lefts):
            @pl.when(col == side)
            def _(left=left):
                for i in range(rows):
                    strip[i * rate : (i + 1) * rate, :] = src[top + i, left : left + rate, :]
        return strip[: padded_rows(rows * rate), :].astype(BF16)

    def paste(dst, top, rows, rate, lefts, value):
        strip[: value.shape[0], :] = value.astype(F32)
        for side, left in enumerate(lefts):
            @pl.when(col == side)
            def _(left=left):
                for i in range(rows):
                    dst[top + i, left : left + rate, :] += strip[i * rate : (i + 1) * rate, :]

    beside = ({"row": 1 - row}, {"col": 1 - col}, {"row": 1 - row, "col": 1 - col})

    def copy(kind, which, src, dst):
        return pltpu.make_async_remote_copy(
            src_ref=src, dst_ref=dst, send_sem=send.at[kind, which], recv_sem=recv.at[kind, which],
            device_id=beside[kind], device_id_type=MESH,
        )

    def edges(index):
        rate = RATES[index]
        pairs = ((vs_ref, vr_ref), (hs_ref, hr_ref), (ds_ref, dr_ref))
        return [
            copy(k, index, src.at[spans[k][rate]], dst.at[spans[k][rate]])
            for k, (src, dst) in enumerate(pairs)
        ]

    @pl.when(step == 0)
    def _():
        barrier = pltpu.get_barrier_semaphore()
        for where in beside:
            pl.semaphore_signal(barrier, inc=1, device_id=where, device_id_type=MESH)
        pl.semaphore_wait(barrier, 3)
        strip[...] = jnp.zeros_like(strip)

    for index, (rate, w_ref) in enumerate(zip(RATES, (wc_ref, wb_ref, wa_ref))):
        tall = n + 2 * rate

        for tap in range(3):
            @pl.when(step == 3 * index + tap)
            def _(rate=rate, w_ref=w_ref, tap=tap, tall=tall):
                top = (2 - tap) * rate * n
                if tap == 0:
                    s_ref[:, : tall * n, :] = jnp.zeros((3, tall * n, outs), F32)
                for across in range(3):
                    s_ref[across, top : top + pix, :] += jnp.dot(
                        f_ref[...], w_ref[0, across], preferred_element_type=F32
                    )

        @pl.when(step == 3 * index + 2)
        def _(rate=rate, tall=tall, index=index):
            t_ref[...] = jnp.zeros_like(t_ref)
            t_ref[:tall, n : 2 * n, :] = s_ref[1, : tall * n, :].reshape(tall, n, outs)
            t_ref[:tall, n + rate : 2 * n + rate, :] += s_ref[0, : tall * n, :].reshape(tall, n, outs)
            t_ref[:tall, n - rate : 2 * n - rate, :] += s_ref[2, : tall * n, :].reshape(tall, n, outs)
            vtop = (1 - row) * (n + rate)
            vs_ref[spans[0][rate], :] = (
                t_ref[pl.ds(vtop, rate), n : 2 * n, :].reshape(rate * n, outs).astype(BF16)
            )
            lefts = (2 * n, n - rate)
            hs_ref[spans[1][rate], :] = cut(t_ref, rate, n, rate, lefts)
            ds_ref[spans[2][rate], :] = cut(t_ref, vtop, rate, rate, lefts)
            for edge in edges(index):
                edge.start()
            acc_ref[3 - index] = t_ref[rate : rate + n, n : 2 * n, :]

    @pl.when(step == 9)
    def _():
        acc_ref[0] = jnp.dot(f_ref[...], wp_ref[...], preferred_element_type=F32).reshape(n, n, outs)
        ft_ref[...] = f_ref[...].T
        for index, rate in enumerate(RATES):
            k = 3 - index
            vtop = (1 - row) * (n - rate)
            v_edge, h_edge, d_edge = edges(index)
            v_edge.wait_recv()
            acc_ref[k, pl.ds(vtop, rate)] += vr_ref[spans[0][rate], :].astype(F32).reshape(rate, n, outs)

            lefts = (n - rate, 0)
            h_edge.wait_recv()
            paste(acc_ref.at[k], 0, n, rate, lefts, hr_ref[spans[1][rate], :])
            d_edge.wait_recv()
            paste(acc_ref.at[k], vtop, rate, rate, lefts, dr_ref[spans[2][rate], :])
        for k in range(4):
            pre = acc_ref[k].reshape(pix, outs)
            joined_ref[:, k * outs : (k + 1) * outs] = (pre * jax.nn.sigmoid(pre)).astype(BF16)
        proj_pre = jnp.dot(joined_ref[...], wq_ref[...], preferred_element_type=F32)
        g_ref[...] = (cot_ref[...].astype(F32) * silu_slope(proj_pre)).astype(BF16)
        for k, out_ref in ((3, d3_ref), (0, d0_ref)):
            d_joined = lax.dot_general(
                g_ref[...], wq_ref[k * outs : (k + 1) * outs, :], (((1,), (1,)), ((), ())),
                preferred_element_type=F32,
            )
            out_ref[...] = (d_joined * silu_slope(acc_ref[k].reshape(pix, outs))).astype(BF16)
            if k == 3:
                part = pl.ds(pl.multiple_of((1 - row) * ((n - REACH) * n), 16), REACH * n)
                v3 = copy(0, 3, d3_ref.at[part], v3_ref)
                v3.start()
                acc_ref[3] = d3_ref[...].astype(F32).reshape(n, n, outs)
                lefts = (n - REACH, 0)
                h3s_ref[...] = cut(acc_ref.at[3], 0, n, REACH, lefts)
                h3 = copy(1, 3, h3s_ref, h3_ref)
                h3.start()
                c3s_ref[...] = cut(acc_ref.at[3], (1 - row) * (n - REACH), REACH, REACH, lefts)
                c3 = copy(2, 3, c3s_ref, c3_ref)
                c3.start()
        chans = joined_ref.shape[1]
        jt_ref[...] = joined_ref[...].T
        g01_ref[:chans, :] = jnp.dot(jt_ref[...], g_ref[...], preferred_element_type=F32)
        g01_ref[chans:, :] = jnp.dot(ft_ref[...], d0_ref[...], preferred_element_type=F32)
        t_ref[...] = jnp.zeros_like(t_ref)
        t_ref[REACH : REACH + n, n : 2 * n, :] = d3_ref[...].astype(F32).reshape(n, n, outs)
        rtop = (1 - row) * (REACH + n)
        lefts = (2 * n, n - REACH)
        v3.wait_recv()
        t_ref[pl.ds(rtop, REACH), n : 2 * n, :] = v3_ref[...].astype(F32).reshape(REACH, n, outs)
        h3.wait_recv()
        paste(t_ref, REACH, n, REACH, lefts, h3_ref[...])
        c3.wait_recv()
        paste(t_ref, rtop, REACH, REACH, lefts, c3_ref[...])
        tall = n + 2 * REACH
        for across in range(3):
            left = n - (across - 1) * REACH
            pb_ref[:, across * outs : (across + 1) * outs] = t_ref[:, left : left + n, :].reshape(tall * n, outs).astype(BF16)
        for index in range(3):
            for edge in edges(index):
                edge.wait_send()
        for edge in (c3, h3, v3):
            edge.wait_send()


def forward(n, f, wc, wb, wa, wp, cot, wq):
    pix, chans = f.shape
    outs = wp.shape[1]
    whole = lambda shape: pl.BlockSpec(shape, lambda t: (0,) * len(shape))
    taps = lambda first: pl.BlockSpec(
        (1, 3, chans, outs), lambda t: (jnp.clip(t - first, 0, 2), 0, 0, 0)
    )
    unused, tops = edge_sizes(n)
    corner = padded_rows(REACH * REACH)
    tall = n + 2 * REACH
    shapes = [((2 * chans, outs), F32), ((chans, pix), BF16), ((tall * n, 3 * outs), BF16)]
    return pl.pallas_call(
        functools.partial(forward_kernel, n),
        grid=(10,),
        out_shape=[jax.ShapeDtypeStruct(s, d) for s, d in shapes],
        in_specs=[whole((pix, chans)), taps(0), taps(3), taps(6), whole((chans, outs)), whole((pix, outs)),
                  whole((chans, outs))],
        out_specs=[whole(s) for s, _ in shapes],
        scratch_shapes=[
            VMEM((3, tall * n, outs), F32),
            VMEM((tall, 3 * n, outs), F32),
            VMEM((4, n, n, outs), F32),
            VMEM((REACH * n, outs), F32),
        ]
        + [VMEM((top, outs), BF16) for top in tops] * 2
        + [
            VMEM((pix, chans), BF16),
            VMEM((chans, pix), BF16),
            VMEM((pix, outs), BF16),
            VMEM((pix, outs), BF16),
            VMEM((pix, outs), BF16),
            VMEM((REACH * n, outs), BF16),
            VMEM((REACH * n, outs), BF16),
            VMEM((corner, outs), BF16),
            VMEM((REACH * n, outs), BF16),
            VMEM((corner, outs), BF16),
            pltpu.SemaphoreType.DMA((3, 4)),
            pltpu.SemaphoreType.DMA((3, 4)),
        ],
        compiler_params=pltpu.CompilerParams(
            collective_id=1, has_side_effects=True, vmem_limit_bytes=LIMIT
        ),
    )(f, wc, wb, wa, wp, cot, wq)


def grads_kernel(n, cap, bs_ref, g01_ref, ft_ref, pb_ref, keep_ref, give_ref):
    core = lax.rem(lax.axis_index("dp"), 2)
    chans, pix = ft_ref.shape
    per = chans // SROWS
    part = SROWS // 4
    keep_ref[...] = jnp.zeros_like(keep_ref)
    give_ref[...] = jnp.zeros_like(give_ref)

    def place(piece, value):
        for s in range(per):
            slot = bs_ref[piece * per + s]
            owner = slot // cap
            for out_ref, side in ((keep_ref, core), (give_ref, 1 - core)):
                @pl.when(lax.rem(owner, 2) == side)
                def _(out_ref=out_ref):
                    for q in range(4):
                        at = s * SROWS + q * part
                        out_ref[owner // 2, q, slot % cap] = value[at : at + part, :].astype(out_ref.dtype)

    for piece in range(2):
        place(piece, g01_ref[piece * chans : (piece + 1) * chans, :])

    def line(above, carry):
        start = pl.multiple_of((2 - above) * (REACH * n), 16)
        value = jnp.dot(ft_ref[...], pb_ref[pl.ds(start, pix), :], preferred_element_type=F32)
        outs = value.shape[1] // 3
        for across in range(3):
            place(2 + 3 * above + across, value[:, across * outs : (across + 1) * outs])
        return carry

    lax.fori_loop(0, 3, line, 0)


def grads(n, cap, pairs, bs, g01, ft, pb):
    outs = g01.shape[1]
    return pl.pallas_call(
        functools.partial(grads_kernel, n, cap),
        out_shape=[jax.ShapeDtypeStruct((pairs, 4, cap, SROWS // 4, outs), d) for d in (F32, BF16)],
        in_specs=[pl.BlockSpec(memory_space=pltpu.SMEM)] + [pl.BlockSpec(memory_space=VMEM)] * 3,
        out_specs=[pl.BlockSpec(memory_space=VMEM)] * 2,
        compiler_params=pltpu.CompilerParams(vmem_limit_bytes=LIMIT),
    )(bs, g01, ft, pb)


def reduce_kernel(pairs, half, held_ref, give_ref, out_ref, keep_ref, r_ref, ax_ref, ay_ref, x1_ref, y1_ref, my_ref, mx_ref,
                  y2_ref, x2_ref, fin_ref, z_ref, send, recv, load):
    row, col, dp = lax.axis_index("row"), lax.axis_index("col"), lax.axis_index("dp")
    core, mine = lax.rem(dp, 2), dp // 2
    depth = keep_ref.shape[2]
    other = {"dp": mine * 2 + 1 - core}
    beside_x = {"row": 1 - row}
    beside_y = {"col": 1 - col}
    zs = [lax.rem(mine + j, pairs) for j in range(pairs)]
    along = [{"dp": zs[j] * 2 + core} for j in range(pairs)]

    fetch = pltpu.make_async_copy(held_ref, keep_ref, load)
    fetch.start()
    barrier = pltpu.get_barrier_semaphore()
    partners = [other, beside_x, beside_y] + along[1:]
    for partner in partners:
        pl.semaphore_signal(barrier, inc=1, device_id=partner, device_id_type=MESH)
    pl.semaphore_wait(barrier, len(partners))

    def copy(kind, j, src, dst, where):
        return pltpu.make_async_remote_copy(
            src_ref=src, dst_ref=dst, send_sem=send.at[kind, j], recv_sem=recv.at[kind, j],
            device_id=where, device_id_type=MESH,
        )

    order = list(range(1, pairs)) + [0]
    low, high = pl.ds(0, half), pl.ds(half, depth - half)
    cores = {j: copy(0, j, give_ref.at[zs[j]], r_ref.at[j], other) for j in order}
    for j in order:
        cores[j].start()
    fetch.wait()
    x1, y1, x2, y2, along_z = {}, {}, {}, {}, {}

    def pair(j, r, c, rows):
        return keep_ref[zs[j], r * 2 + c, rows, :] + r_ref[j, r * 2 + c, rows, :].astype(F32)

    def first(j):
        cores[j].wait_recv()
        for k in range(2):
            ax_ref[j, k] = pair(j, 1 - row, k, low).astype(BF16)
            ay_ref[j, k] = pair(j, k, 1 - col, high).astype(BF16)
        x1[j] = copy(1, j, ax_ref.at[j], x1_ref.at[j], beside_x)
        y1[j] = copy(2, j, ay_ref.at[j], y1_ref.at[j], beside_y)
        x1[j].start()
        y1[j].start()

    def second(j):
        x1[j].wait_recv()
        my_ref[j] = (pair(j, row, 1 - col, low) + x1_ref[j, 1 - col].astype(F32)).astype(BF16)
        y2[j] = copy(3, j, my_ref.at[j], y2_ref.at[j], beside_y)
        y2[j].start()
        y1[j].wait_recv()
        mx_ref[j] = (pair(j, 1 - row, col, high) + y1_ref[j, 1 - row].astype(F32)).astype(BF16)
        x2[j] = copy(4, j, mx_ref.at[j], x2_ref.at[j], beside_x)
        x2[j].start()

    def third(j):
        y2[j].wait_recv()
        x2[j].wait_recv()
        lower = pair(j, row, col, low) + x1_ref[j, col].astype(F32) + y2_ref[j].astype(F32)
        upper = pair(j, row, col, high) + y1_ref[j, row].astype(F32) + x2_ref[j].astype(F32)
        if j == 0:
            out_ref[low, :] = lower
            out_ref[high, :] = upper
        else:
            fin_ref[j, low, :] = lower.astype(BF16)
            fin_ref[j, high, :] = upper.astype(BF16)
            along_z[j] = copy(5, j, fin_ref.at[j], z_ref.at[j], along[j])
            along_z[j].start()

    for at in range(pairs + 2):
        if at < pairs:
            first(order[at])
        if 1 <= at <= pairs:
            second(order[at - 1])
        if at >= 2:
            third(order[at - 2])
    for j in order[:-1]:
        along_z[j].wait_recv()
        out_ref[...] += z_ref[j].astype(F32)
    for j in order:
        for group in (cores, x1, y1, x2, y2):
            group[j].wait_send()
        if j:
            along_z[j].wait_send()


def reduce_scatter(keep, give):
    pairs, quarters, depth, outs = keep.shape
    half = (depth // 16 + 1) // 2 * 16
    rest = depth - half
    buf = lambda *shape: VMEM(shape + (outs,), BF16)
    return pl.pallas_call(
        functools.partial(reduce_kernel, pairs, half),
        out_shape=jax.ShapeDtypeStruct((depth, outs), F32),
        in_specs=[pl.BlockSpec(memory_space=pl.ANY)] * 2,
        out_specs=pl.BlockSpec(memory_space=VMEM),
        scratch_shapes=[
            VMEM(keep.shape, F32),
            buf(pairs, quarters, depth),
            buf(pairs, 2, half),
            buf(pairs, 2, rest),
            buf(pairs, 2, half),
            buf(pairs, 2, rest),
            buf(pairs, half),
            buf(pairs, rest),
            buf(pairs, half),
            buf(pairs, rest),
            buf(pairs, depth),
            buf(pairs, depth),
            pltpu.SemaphoreType.DMA((6, pairs)),
            pltpu.SemaphoreType.DMA((6, pairs)),
            pltpu.SemaphoreType.DMA,
        ],
        compiler_params=pltpu.CompilerParams(
            collective_id=0, has_side_effects=True, vmem_limit_bytes=LIMIT
        ),
    )(keep, give)


def shards(features, cotangent, w_point, w_rate_a, w_rate_b, w_rate_c, w_proj, bucket_slot):
    n = features.shape[1]
    chans = features.shape[3]
    outs = w_point.shape[1]
    pix = n * n
    f = features.reshape(pix, chans)
    cot = cotangent.reshape(pix, outs)
    replicas = lax.axis_size("dp")
    nslice = bucket_slot.shape[0]
    cap = nslice // replicas + 1
    g01, ft, pb = forward(n, f, w_rate_c, w_rate_b, w_rate_a, w_point, cot, w_proj)
    keep, give = grads(n, cap, replicas // 2, bucket_slot, g01, ft, pb)
    shape = (replicas // 2, 4, cap * (SROWS // 4), outs)
    total = reduce_scatter(keep.reshape(shape), give.reshape(shape))
    return total.reshape(cap, SROWS // 4 * outs)


def solution(mesh):
    placed = (
        P("dp", "row", "col", None),
        P("dp", "row", "col", None),
        P(),
        P(),
        P(),
        P(),
        P(),
        P(),
    )
    return jax.shard_map(
        shards, mesh=mesh, in_specs=placed, out_specs=P("dp", ("row", "col")), check_vma=False
    )
```
